512 devices in a mesh: dp: 32 (over z, x), expert: 16 (over y, core).
Axes of the slice: x: 4, y: 8, z: 8, core: 2. Of those that a mesh axis runs over, the one named last changes fastest.
Arguments:
- tokens: bfloat16 [131072, 1024], P(('dp', 'expert')), may hold values from -6 to 6
- grad_out: bfloat16 [131072, 1024], P(('dp', 'expert')), may hold values from -6 to 6
- combine: bfloat16 [131072, 8], P(('dp', 'expert')), may hold values from 0.049804688 to 1
- expert_ids: int32 [131072, 8], P(('dp', 'expert')), may hold values from 0 to 127, as said below
- slots: int32 [131072, 8], P(('dp', 'expert')), may hold values from -1 to 31, as said below
- w_gate: bfloat16 [16, 1024, 384], P('expert'), may hold values from -0.1875 to 0.1875
- w_up: bfloat16 [16, 1024, 384], P('expert'), may hold values from -0.1875 to 0.1875
- w_down: bfloat16 [16, 384, 1024], P('expert'), may hold values from -0.3125 to 0.3125
Outputs:
- grad_tokens: bfloat16 [131072, 1024], P(('dp', 'expert'))
- grad_combine: bfloat16 [131072, 8], P(('dp', 'expert'))
- grad_w_gate: float32 [16, 1024, 384], P('expert', 'dp')
- grad_w_up: float32 [16, 1024, 384], P('expert', 'dp')
- grad_w_down: float32 [16, 384, 1024], P('expert', None, 'dp')
The draws below stay inside these ranges and needn't reach their ends.
Inputs may be any that keep to these rules, and one draw needn't show every extreme that they name: `expert_ids`: each row names 8 different experts; experts numbered 16 or above are not computed here. `slots`: a choice of an expert below 16 has as slot the number of earlier rows of the same device (block of 256 rows) that chose the same expert, if that number is below 32; every other choice has -1. In every group of 16 consecutive devices' rows, some expert has 32 active choices from every device of the group.
All inputs are finite; a program needn't handle non-finite values.
Results may differ from the reference program's by a relative error of at most 0.02.
Values may be sent and summed in bfloat16 or wider, within the bound.
No kernel may reach another device: no remote copies, remote signals or barrier semaphores. Data moves between devices by JAX's collectives and lax.ppermute only.
A program may use at most 64 MiB of HBM per device.

```python
import math
import jax
import jax.numpy as jnp
from jax import lax

D = 1024
FF = 384
EXPERTS = 128
TOP = 8
TOK_DEV = 256
CAP = 32
EXPERTS_WIN = 16
TOKENS = 131072
N_DP = 32
N_EXPERT = 16


def routing(key):
    group_rows = TOK_DEV * N_EXPERT
    groups = TOKENS // group_rows
    hottest = jax.random.randint(jax.random.fold_in(key, 11), (groups,), 0, EXPERTS_WIN)
    hot_rows = jnp.repeat(hottest, group_rows, total_repeat_length=TOKENS)
    columns = jnp.arange(EXPERTS, dtype=jnp.int32)
    scores = jax.random.randint(jax.random.fold_in(key, 12), (TOKENS, EXPERTS), 0, 1 << 20) * EXPERTS + columns[None, :]
    scores = jnp.where(columns[None, :] == hot_rows[:, None], 1 << 30, scores)
    unused, chosen = lax.top_k(scores, TOP)
    chosen = chosen.astype(jnp.int32)
    row_index = jnp.arange(TOKENS, dtype=jnp.int32)[:, None]
    picked = jnp.zeros((TOKENS, EXPERTS), jnp.int32).at[row_index, chosen].set(1)
    blocked = picked.reshape(TOKENS // TOK_DEV, TOK_DEV, EXPERTS)
    earlier = (jnp.cumsum(blocked, axis=1) - blocked).reshape(TOKENS, EXPERTS)
    ranking = jnp.take_along_axis(earlier, chosen, axis=1)
    chosen_slots = jnp.where((chosen < EXPERTS_WIN) & (ranking < CAP), ranking, -1).astype(jnp.int32)
    return (chosen, chosen_slots)


def draw_expert_ids(key, part):
    chosen, chosen_slots = routing(key)
    return chosen


def draw_slots(key, part):
    chosen, chosen_slots = routing(key)
    return chosen_slots


def shard_levels(rng, shape, shards, smallest, top_value):
    gain, own = 1.0, jax.random.fold_in(rng, 6)
    for dim, parts in shards:
        steps = jnp.exp(jax.random.uniform(jax.random.fold_in(own, dim), (parts,), jnp.float32, smallest / len(shards), top_value / len(shards)))
        gain = gain * jnp.repeat(steps, shape[dim] // parts).reshape([-1 if axis == dim else 1 for axis in range(len(shape))])
    return gain


def centred(rng, extent, spread, most, cuts=(), kind=jnp.bfloat16):
    entries = spread * jax.random.normal(rng, extent, jnp.float32)
    if cuts:
        entries = entries * shard_levels(rng, extent, cuts, -0.22, 0.18)
    return jnp.clip(entries, -most, most).astype(kind)


def setup_inputs(seed: int = 0) -> dict:
    seeds = jax.random.split(jax.random.key(seed), 9)
    return {
        "tokens": centred(seeds[0], (TOKENS, D), 1.0, 6.0, ((0, 512),)),
        "grad_out": centred(seeds[1], (TOKENS, D), 1.0, 6.0, ((0, 512),)),
        "combine": jnp.clip(jnp.exp(math.log(1.0) - 2.9996462 * jax.random.uniform(seeds[2], (TOKENS, TOP), jnp.float32) ** shard_levels(seeds[2], (TOKENS, TOP), ((0, 512),), -0.2, 0.2)), 0.049804688, 1.0).astype(jnp.bfloat16),
        "expert_ids": draw_expert_ids(jax.random.fold_in(seeds[8], 71), 0),
        "slots": draw_slots(jax.random.fold_in(seeds[8], 71), 0),
        "w_gate": centred(seeds[5], (EXPERTS_WIN, D, FF), D ** -0.5, 0.1875, ((0, 16),)),
        "w_up": centred(seeds[6], (EXPERTS_WIN, D, FF), D ** -0.5, 0.1875, ((0, 16),)),
        "w_down": centred(seeds[7], (EXPERTS_WIN, FF, D), FF ** -0.5, 0.3125, ((0, 16),)),
    }


def silu_slope(values):
    sig = jax.nn.sigmoid(values)
    return sig * (1.0 + values * (1.0 - sig))


def expert_pass(buffer_x, buffer_g, buffer_c, w_gate, w_up, w_down):
    xf = buffer_x.astype(jnp.float32)
    wgf = w_gate.astype(jnp.float32)
    wuf = w_up.astype(jnp.float32)
    wdf = w_down.astype(jnp.float32)
    gate_pre = jnp.einsum("erd,edf->erf", xf, wgf)
    up_pre = jnp.einsum("erd,edf->erf", xf, wuf)
    gate_act = jax.nn.silu(gate_pre)
    hidden = (gate_act * up_pre).astype(jnp.bfloat16)
    output = jnp.einsum("erf,efd->erd", hidden.astype(jnp.float32), wdf)
    row_combine = jnp.sum(buffer_g.astype(jnp.float32) * output, axis=-1).astype(jnp.bfloat16)
    grad_row = (buffer_c.astype(jnp.float32)[..., None] * buffer_g.astype(jnp.float32)).astype(jnp.bfloat16)
    grad_hidden = jnp.einsum("erd,efd->erf", grad_row.astype(jnp.float32), wdf)
    grad_gate = (grad_hidden * up_pre * silu_slope(gate_pre)).astype(jnp.bfloat16)
    grad_up = (grad_hidden * gate_act).astype(jnp.bfloat16)
    row_input = jnp.einsum("erf,edf->erd", grad_gate.astype(jnp.float32), wgf)
    row_input = (row_input + jnp.einsum("erf,edf->erd", grad_up.astype(jnp.float32), wuf)).astype(jnp.bfloat16)
    part_gate = jnp.einsum("erd,erf->edf", xf, grad_gate.astype(jnp.float32))
    part_up = jnp.einsum("erd,erf->edf", xf, grad_up.astype(jnp.float32))
    part_down = jnp.einsum("erf,erd->efd", hidden.astype(jnp.float32), grad_row.astype(jnp.float32))
    return row_input, row_combine, part_gate, part_up, part_down


def rounded(values):
    return lax.optimization_barrier(values.astype(jnp.bfloat16)).astype(jnp.float32)


def reference(tokens, grad_out, combine, expert_ids, slots, w_gate, w_up, w_down):
    group_rows = N_EXPERT * TOK_DEV
    buffer_rows = N_EXPERT * CAP
    total_rows = EXPERTS_WIN * buffer_rows

    def one_group(totals, pieces):
        x_group, g_group, c_group, id_group, slot_group = pieces
        source = (jnp.arange(group_rows, dtype=jnp.int32) // TOK_DEV)[:, None]
        active = slot_group >= 0
        target = jnp.where(active, id_group * buffer_rows + source * CAP + slot_group, total_rows).astype(jnp.int32)
        target_flat = target.reshape(-1)
        buffer_x = jnp.zeros((total_rows, D), jnp.bfloat16).at[target_flat].set(jnp.repeat(x_group, TOP, axis=0), mode="drop")
        buffer_g = jnp.zeros((total_rows, D), jnp.bfloat16).at[target_flat].set(jnp.repeat(g_group, TOP, axis=0), mode="drop")
        buffer_c = jnp.zeros((total_rows,), jnp.bfloat16).at[target_flat].set(c_group.reshape(-1), mode="drop")
        row_input, row_combine, part_gate, part_up, part_down = expert_pass(
            buffer_x.reshape(EXPERTS_WIN, buffer_rows, D), buffer_g.reshape(EXPERTS_WIN, buffer_rows, D),
            buffer_c.reshape(EXPERTS_WIN, buffer_rows), w_gate, w_up, w_down)
        clipped = jnp.minimum(target, total_rows - 1).astype(jnp.int32)
        picked = row_input.reshape(total_rows, D)[clipped].astype(jnp.float32)
        grad_group = jnp.sum(jnp.where(active[..., None], picked, 0.0), axis=1).astype(jnp.bfloat16)
        comb_group = jnp.where(active, row_combine.reshape(total_rows)[clipped], jnp.zeros((), jnp.bfloat16))
        new_totals = (totals[0] + rounded(part_gate), totals[1] + rounded(part_up), totals[2] + rounded(part_down))
        return new_totals, (grad_group, comb_group)

    start = (jnp.zeros((EXPERTS_WIN, D, FF), jnp.float32), jnp.zeros((EXPERTS_WIN, D, FF), jnp.float32),
             jnp.zeros((EXPERTS_WIN, FF, D), jnp.float32))
    pieces = (tokens.reshape(N_DP, group_rows, D), grad_out.reshape(N_DP, group_rows, D),
              combine.reshape(N_DP, group_rows, TOP), expert_ids.reshape(N_DP, group_rows, TOP),
              slots.reshape(N_DP, group_rows, TOP))
    totals, (grad_groups, comb_groups) = lax.scan(one_group, start, pieces)
    grad_tokens = grad_groups.reshape(TOKENS, D)
    grad_combine = comb_groups.reshape(TOKENS, TOP)
    return grad_tokens, grad_combine, totals[0], totals[1], totals[2]
```

```python
import functools

import jax
import jax.numpy as jnp
from jax import lax
from jax.experimental import pallas as pl
from jax.experimental.pallas import tpu as pltpu
from jax.sharding import Mesh, PartitionSpec as P

X_CHIPS = 4
LANES = 128
F32 = jnp.float32
BF16 = jnp.bfloat16
TN = (((0,), (0,)), ((), ()))
NT = (((1,), (1,)), ((), ()))


def dot(a, b, dims=(((1,), (0,)), ((), ()))):
    return lax.dot_general(a, b, dims, preferred_element_type=F32)


def positions(ids, slots, experts, half_rows):
    half = jnp.where(slots >= half_rows, 1, 0)
    row = half * (experts * half_rows) + ids * half_rows + (slots - half * half_rows)
    return jnp.where(slots >= 0, row, -1)


def dispatch_kernel(experts, half_rows, x_ref, g_ref, c_ref, id_ref, slot_ref, out_ref):
    tokens, width = x_ref.shape
    block = experts * half_rows
    pos = positions(id_ref[...], slot_ref[...], experts, half_rows)
    weights = c_ref[...].astype(F32)
    column = lax.broadcasted_iota(jnp.int32, (tokens, 2 * block), 1)
    routed = jnp.zeros((tokens, 2 * block), F32)
    scaled = jnp.zeros((tokens, 2 * block), F32)
    for k in range(pos.shape[1]):
        match = pos[:, k : k + 1] == column
        routed = jnp.where(match, 1.0, routed)
        scaled = jnp.where(match, weights[:, k : k + 1], scaled)
    routed = routed.astype(BF16)
    scaled = scaled.astype(BF16)
    lane = lax.broadcasted_iota(jnp.int32, (tokens, LANES), 1)
    coded = jnp.zeros((block, LANES), F32)
    for h in range(2):
        pick = routed[:, h * block : (h + 1) * block]
        out_ref[:, h * width : (h + 1) * width] = dot(pick, x_ref[...], TN).astype(BF16)
        out_ref[:, (2 + h) * width : (3 + h) * width] = dot(pick, g_ref[...], TN).astype(BF16)
        mine = jnp.where(lane // (LANES // 2) == h, 1.0, 0.0).astype(BF16)
        coded = coded + dot(scaled[:, h * block : (h + 1) * block], mine, TN)
    out_ref[:, 4 * width :] = coded.astype(BF16)


def expert_kernel(chunk, rows_ref, wgu_ref, wd_ref, back_ref, own_ref, next_ref, far_ref, prev_ref, x_all, r_all, act_all, part):
    block = rows_ref.shape[0]
    hidden_units, width = wd_ref.shape
    wgu = wgu_ref[...]
    wd = wd_ref[...]
    lane = lax.broadcasted_iota(jnp.int32, (block, LANES), 1)
    sums = jnp.zeros((block, LANES), F32)
    for h in range(2):
        x = rows_ref[:, h * width : (h + 1) * width]
        g = rows_ref[:, (2 + h) * width : (3 + h) * width]
        at = 4 * width + h * (LANES // 2)
        c = rows_ref[:, at : at + 1].astype(F32)
        pre = dot(x, wgu)
        gate, up = pre[:, :hidden_units], pre[:, hidden_units:]
        sig = 1.0 / (1.0 + jnp.exp(-gate))
        act = gate * sig
        hidden = (act * up).astype(BF16)
        g_hidden = dot(g, wd, NT)
        row_combine = jnp.sum(hidden.astype(F32) * g_hidden, axis=1, keepdims=True)
        sums = jnp.where(lane // (LANES // 2) == h, row_combine, sums)
        grad_hidden = c * g_hidden
        grad_gate = (grad_hidden * up * (sig * (1.0 + gate * (1.0 - sig)))).astype(BF16)
        grad_up = (grad_hidden * act).astype(BF16)
        lo, hi = h * block, (h + 1) * block
        x_all[lo:hi, :] = x
        r_all[lo:hi, :] = (c * g.astype(F32)).astype(BF16)
        act_all[lo:hi, :hidden_units] = grad_gate
        act_all[lo:hi, hidden_units : 2 * hidden_units] = grad_up
        act_all[lo:hi, 2 * hidden_units :] = hidden
        back_ref[:, h * width : (h + 1) * width] = dot(act_all[lo:hi, : 2 * hidden_units], wgu, NT).astype(BF16)
    back_ref[:, 2 * width :] = sums.astype(BF16)
    step = 256
    for d in range(0, width, step):
        upper = dot(x_all[:, d : d + step], act_all[:, : 2 * hidden_units], TN).astype(BF16)
        lower = dot(r_all[:, d : d + step], act_all[:, 2 * hidden_units :], TN).astype(BF16)
        for j in range(0, step, chunk):
            part[(d + j) // chunk, :, : 2 * hidden_units] = upper[j : j + chunk]
            part[(d + j) // chunk, :, 2 * hidden_units :] = lower[j : j + chunk]
    me = lax.axis_index("x")
    for k, ref in enumerate((own_ref, next_ref, far_ref, prev_ref)):
        x_to = lax.rem(me + k, X_CHIPS)
        for z in range(width // chunk // X_CHIPS):
            ref[z * chunk : (z + 1) * chunk, :] = part[z * X_CHIPS + x_to]


def combine_kernel(experts, half_rows, back_ref, id_ref, slot_ref, grad_ref, comb_ref):
    tokens, width = grad_ref.shape
    block = experts * half_rows
    pos = positions(id_ref[...], slot_ref[...], experts, half_rows)
    column = lax.broadcasted_iota(jnp.int32, (tokens, 2 * block), 1)
    coded = jnp.transpose(back_ref[:, 2 * width :].astype(F32))
    sums = jnp.concatenate([coded[0:1, :], coded[LANES // 2 : LANES // 2 + 1, :]], axis=1)
    routed = jnp.zeros((tokens, 2 * block), F32)
    choice = lax.broadcasted_iota(jnp.int32, (tokens, pos.shape[1]), 1)
    comb = jnp.zeros((tokens, pos.shape[1]), F32)
    for k in range(pos.shape[1]):
        match = pos[:, k : k + 1] == column
        routed = jnp.where(match, 1.0, routed)
        value = jnp.sum(jnp.where(match, sums, 0.0), axis=1, keepdims=True)
        comb = jnp.where(choice == k, value, comb)
    comb_ref[...] = comb.astype(BF16)
    routed = routed.astype(BF16)
    grad = dot(routed[:, :block], back_ref[:, :width]) + dot(routed[:, block:], back_ref[:, width : 2 * width])
    grad_ref[...] = grad.astype(BF16)


def total_kernel(q_ref, gate_ref, up_ref, down_ref):
    hidden_units = gate_ref.shape[1]
    total = jnp.sum(q_ref[...].astype(F32), axis=0)
    gate_ref[...] = total[:, :hidden_units]
    up_ref[...] = total[:, hidden_units : 2 * hidden_units]
    down_ref[...] = jnp.transpose(total[:, 2 * hidden_units :])


def call(kernel, out_shape, args, flops=0, scratch=(), limit=24):
    moved = sum(a.size * a.dtype.itemsize for a in (*args, *out_shape))
    return pl.pallas_call(
        kernel,
        out_shape=out_shape,
        in_specs=[pl.BlockSpec(memory_space=pltpu.VMEM)] * len(args),
        out_specs=[pl.BlockSpec(memory_space=pltpu.VMEM)] * len(out_shape),
        scratch_shapes=scratch,
        compiler_params=pltpu.CompilerParams(vmem_limit_bytes=limit << 20),
        cost_estimate=pl.CostEstimate(flops=flops, bytes_accessed=moved, transcendentals=0),
    )(*args)


def shape(*dims, dtype=BF16):
    return jax.ShapeDtypeStruct(dims, dtype)


def shards(tokens, grad_out, combine, expert_ids, slots, w_gate, w_up, w_down):
    tok_rows, width = tokens.shape
    hidden_units = w_gate.shape[2]
    experts = lax.axis_size("expert")
    z_chips = lax.axis_size("z")
    half_rows = tok_rows // 16
    block = experts * half_rows
    chunk = width // (z_chips * X_CHIPS)
    wgu = jnp.concatenate([w_gate[0], w_up[0]], axis=1)
    wd = w_down[0]

    (sent,) = call(
        functools.partial(dispatch_kernel, experts, half_rows),
        [shape(block, 4 * width + LANES)],
        (tokens, grad_out, combine, expert_ids, slots),
        flops=8 * tok_rows * block * width,
    )
    got = lax.all_to_all(sent, "expert", split_axis=0, concat_axis=0, tiled=True)
    cols = 3 * hidden_units
    piece = shape(z_chips * chunk, cols)
    back, own, nxt, far, prv = call(
        functools.partial(expert_kernel, chunk),
        [shape(block, 2 * width + LANES), piece, piece, piece, piece],
        (got, wgu, wd),
        flops=16 * 2 * block * width * hidden_units,
        scratch=[
            pltpu.VMEM((2 * block, width), BF16),
            pltpu.VMEM((2 * block, width), BF16),
            pltpu.VMEM((2 * block, cols), BF16),
            pltpu.VMEM((width // chunk, chunk, cols), BF16),
        ],
        limit=40,
    )
    returned = lax.all_to_all(back, "expert", split_axis=0, concat_axis=0, tiled=True)

    def shift(values, k):
        return lax.ppermute(values, "x", [(i, (i + k) % X_CHIPS) for i in range(X_CHIPS)])

    from_far = shift(far, 2)
    from_prev = shift(nxt, 1)
    from_next = shift(prv, 3)
    summed = own.astype(F32) + from_prev.astype(F32) + from_next.astype(F32) + from_far.astype(F32)
    summed = summed.astype(BF16)
    summed, returned = lax.optimization_barrier((summed, returned))
    pieces = lax.all_to_all(summed, "z", split_axis=0, concat_axis=0, tiled=True)
    grad_tokens, grad_combine = call(
        functools.partial(combine_kernel, experts, half_rows),
        [shape(tok_rows, width), shape(*slots.shape)],
        (returned, expert_ids, slots),
        flops=4 * tok_rows * block * width,
    )
    grad_gate, grad_up, grad_down = call(
        total_kernel,
        [
            shape(chunk, hidden_units, dtype=F32),
            shape(chunk, hidden_units, dtype=F32),
            shape(hidden_units, chunk, dtype=F32),
        ],
        (pieces.reshape(z_chips, chunk, cols),),
    )
    return grad_tokens, grad_combine, grad_gate[None], grad_up[None], grad_down[None]


def solution(mesh):
    groups, experts = mesh.devices.shape
    split = Mesh(mesh.devices.reshape(groups // X_CHIPS, X_CHIPS, experts), ("z", "x", "expert"))
    dp = ("z", "x")
    rows = P((*dp, "expert"), None)
    weight = P("expert", None, None)
    return jax.shard_map(
        shards,
        mesh=split,
        in_specs=(rows,) * 5 + (weight,) * 3,
        out_specs=(rows, rows, P("expert", dp, None), P("expert", dp, None), P("expert", None, dp)),
        check_vma=False,
    )
```

```python
import functools

import jax
import jax.numpy as jnp
from jax import lax
from jax.experimental import pallas as pl
from jax.experimental.pallas import tpu as pltpu
from jax.sharding import Mesh, PartitionSpec as P

X_CHIPS = 4
LANES = 128
PACK = 4
CODE = LANES // PACK
FIRST = (0, 2, 1, 3)
F32 = jnp.float32
BF16 = jnp.bfloat16
NN = (((1,), (0,)), ((), ()))
TN = (((0,), (0,)), ((), ()))
NT = (((1,), (1,)), ((), ()))


def dot(a, b, dims=NN):
    return lax.dot_general(a, b, dims, preferred_element_type=F32)


def positions(ids, slots, experts, per):
    group = slots // per
    row = group * (experts * per) + ids * per + (slots - group * per)
    return jnp.where(slots >= 0, row, -1)


def dispatch_kernel(experts, per, x_hbm, g_hbm, c_hbm, id_hbm, slot_hbm, out_hbm,
                    x_ref, g_ref, c_ref, id_ref, slot_ref, out_ref, sems, out_sems):
    tokens, width = x_ref.shape
    block = experts * per
    rows = PACK * block
    fetches = [
        pltpu.make_async_copy(source, ref, sems.at[i])
        for i, (source, ref) in enumerate(
            ((id_hbm, id_ref), (slot_hbm, slot_ref), (c_hbm, c_ref), (x_hbm, x_ref), (g_hbm, g_ref))
        )
    ]
    for fetch in fetches:
        fetch.start()
    fetch_x, fetch_g = fetches[3:]
    for fetch in fetches[:3]:
        fetch.wait()
    pos = positions(id_ref[...], slot_ref[...], experts, per)
    weights = c_ref[...].astype(F32)
    index = lax.broadcasted_iota(jnp.int32, (rows, tokens), 0)
    routed = jnp.zeros((rows, tokens), F32)
    scaled = jnp.zeros((rows, tokens), F32)
    for k in range(pos.shape[0]):
        match = index == pos[k : k + 1, :]
        routed = jnp.where(match, 1.0, routed)
        scaled = jnp.where(match, weights[k : k + 1, :], scaled)
    routed = routed.astype(BF16)
    code = jnp.sum(scaled, axis=1, keepdims=True)
    lane = lax.broadcasted_iota(jnp.int32, (block, LANES), 1)
    coded = jnp.zeros((block, LANES), F32)
    for q in range(PACK):
        coded = jnp.where(lane // CODE == q, code[q * block : (q + 1) * block], coded)
    out_ref[:, 2 * PACK * width :] = coded.astype(BF16)
    fetch_x.wait()
    sent = dot(routed, x_ref[...]).astype(BF16)
    for q in range(PACK):
        out_ref[:, q * width : (q + 1) * width] = sent[q * block : (q + 1) * block]
    half = PACK * width
    first = pltpu.make_async_copy(out_ref.at[:, :half], out_hbm.at[:, :half], out_sems.at[0])
    first.start()
    fetch_g.wait()
    sent = dot(routed, g_ref[...]).astype(BF16)
    for q in range(PACK):
        out_ref[:, half + q * width : half + (q + 1) * width] = sent[q * block : (q + 1) * block]
    second = pltpu.make_async_copy(out_ref.at[:, half:], out_hbm.at[:, half:], out_sems.at[1])
    second.start()
    first.wait()
    second.wait()


def expert_kernel(rows_ref, wg_ref, wu_ref, wd_ref, back_ref, *rest):
    pieces, (x_all, g_all, act_all, part) = rest[:-4], rest[-4:]
    block = back_ref.shape[0]
    hidden_units, width = wd_ref.shape
    rows = PACK * block
    for q in range(PACK):
        x_all[q * block : (q + 1) * block, :] = rows_ref[:, q * width : (q + 1) * width]
        g_all[q * block : (q + 1) * block, :] = rows_ref[:, (PACK + q) * width : (PACK + q + 1) * width]
    lane = lax.broadcasted_iota(jnp.int32, (block, LANES), 1)
    sums = jnp.zeros((block, LANES), F32)
    step = rows // 2
    for lo in range(0, rows, step):
        hi = lo + step
        g = g_all[lo:hi, :]
        c = jnp.concatenate(
            [
                rows_ref[:, 2 * PACK * width + q * CODE : 2 * PACK * width + q * CODE + 1].astype(F32)
                for q in range(lo // block, hi // block)
            ],
            axis=0,
        )
        gate = dot(x_all[lo:hi, :], wg_ref[...])
        up = dot(x_all[lo:hi, :], wu_ref[...])
        sig = 1.0 / (1.0 + jnp.exp(-gate))
        act = gate * sig
        hidden = (act * up).astype(BF16)
        g_hidden = dot(g, wd_ref[...], NT)
        row_combine = jnp.sum(hidden.astype(F32) * g_hidden, axis=1, keepdims=True)
        for q in range(lo // block, hi // block):
            sums = jnp.where(lane // CODE == q, row_combine[q * block - lo : (q + 1) * block - lo], sums)
        grad_hidden = c * g_hidden
        g_all[lo:hi, :] = (c * g.astype(F32)).astype(BF16)
        act_all[lo:hi, :hidden_units] = (grad_hidden * up * (sig * (1.0 + gate * (1.0 - sig)))).astype(BF16)
        act_all[lo:hi, hidden_units : 2 * hidden_units] = (grad_hidden * act).astype(BF16)
        act_all[lo:hi, 2 * hidden_units :] = hidden
    back_ref[:, PACK * width :] = sums.astype(BF16)
    grad = dot(act_all[:, :hidden_units], wg_ref[...], NT)
    grad = (grad + dot(act_all[:, hidden_units : 2 * hidden_units], wu_ref[...], NT)).astype(BF16)
    for q in range(PACK):
        back_ref[:, q * width : (q + 1) * width] = grad[q * block : (q + 1) * block]
    step = 256
    chunk = part.shape[1]
    for d in range(0, width, step):
        upper = dot(x_all[:, d : d + step], act_all[:, : 2 * hidden_units], TN).astype(BF16)
        lower = dot(g_all[:, d : d + step], act_all[:, 2 * hidden_units :], TN).astype(BF16)
        for j in range(0, step, chunk):
            part[(d + j) // chunk, :, : 2 * hidden_units] = upper[j : j + chunk]
            part[(d + j) // chunk, :, 2 * hidden_units :] = lower[j : j + chunk]
    here = lax.axis_index("x")
    for dx, ref in zip(FIRST, pieces, strict=True):
        x_to = lax.rem(here + dx, X_CHIPS)
        for z in range(ref.shape[0]):
            ref[z] = part[z * X_CHIPS + x_to]


def partial_kernel(*refs):
    total = refs[0][...].astype(F32)
    for ref in refs[1:-1]:
        total = total + ref[...].astype(F32)
    refs[-1][...] = total.astype(BF16)


def combine_kernel(experts, per, back_ref, id_ref, slot_ref, grad_ref, comb_ref):
    tokens, width = grad_ref.shape
    block = experts * per
    rows = PACK * block
    pos = positions(id_ref[...], slot_ref[...], experts, per)
    index = lax.broadcasted_iota(jnp.int32, (rows, tokens), 0)
    code = jnp.concatenate(
        [
            back_ref[:, PACK * width + q * CODE : PACK * width + q * CODE + 1].astype(F32)
            for q in range(PACK)
        ],
        axis=0,
    )
    routed = jnp.zeros((rows, tokens), F32)
    choice = lax.broadcasted_iota(jnp.int32, pos.shape, 0)
    comb = jnp.zeros(pos.shape, F32)
    for k in range(pos.shape[0]):
        match = index == pos[k : k + 1, :]
        routed = jnp.where(match, 1.0, routed)
        value = jnp.sum(jnp.where(match, code, 0.0), axis=0, keepdims=True)
        comb = jnp.where(choice == k, value, comb)
    comb_ref[...] = comb.astype(BF16)
    routed = routed.astype(BF16)
    grad = jnp.zeros((tokens, width), F32)
    for q in range(PACK):
        grad = grad + dot(routed[q * block : (q + 1) * block], back_ref[:, q * width : (q + 1) * width], TN)
    grad_ref[...] = grad.astype(BF16)


def total_kernel(parts_ref, gate_ref, up_ref, down_ref):
    hidden_units = gate_ref.shape[1]
    total = jnp.sum(parts_ref[...].astype(F32), axis=0)
    gate_ref[...] = total[:, :hidden_units]
    up_ref[...] = total[:, hidden_units : 2 * hidden_units]
    down_ref[...] = total[:, 2 * hidden_units :]


def call(kernel, out_shape, args, flops=0, scratch=(), limit=24, ins="", outs=""):
    moved = sum(a.size * a.dtype.itemsize for a in (*args, *out_shape))

    def specs(letters, count):
        letters = letters.ljust(count, "v")
        return [pl.BlockSpec(memory_space=pltpu.HBM if c == "h" else pltpu.VMEM) for c in letters]

    return pl.pallas_call(
        kernel,
        out_shape=out_shape,
        in_specs=specs(ins, len(args)),
        out_specs=specs(outs, len(out_shape)),
        scratch_shapes=scratch,
        compiler_params=pltpu.CompilerParams(vmem_limit_bytes=limit << 20),
        cost_estimate=pl.CostEstimate(flops=flops, bytes_accessed=moved, transcendentals=0),
    )(*args)


def shape(*dims, dtype=BF16):
    return jax.ShapeDtypeStruct(dims, dtype)


def shards(tokens, grad_out, combine, expert_ids, slots, w_gate, w_up, w_down):
    tok_rows, width = tokens.shape
    hidden_units = w_gate.shape[2]
    experts = lax.axis_size("expert")
    z_chips = lax.axis_size("z")
    per = tok_rows // 8 // PACK
    block = experts * per
    rows = PACK * block
    chunk = width // (z_chips * X_CHIPS)
    cols = 3 * hidden_units
    ids_t, slots_t, combine_t = expert_ids.T, slots.T, combine.T

    (sent,) = call(
        functools.partial(dispatch_kernel, experts, per),
        [shape(block, 2 * PACK * width + LANES)],
        (tokens, grad_out, combine_t, ids_t, slots_t),
        flops=4 * tok_rows * rows * width,
        scratch=[
            pltpu.VMEM((tok_rows, width), BF16),
            pltpu.VMEM((tok_rows, width), BF16),
            pltpu.VMEM(combine_t.shape, BF16),
            pltpu.VMEM(ids_t.shape, jnp.int32),
            pltpu.VMEM(slots_t.shape, jnp.int32),
            pltpu.VMEM((block, 2 * PACK * width + LANES), BF16),
            pltpu.SemaphoreType.DMA((5,)),
            pltpu.SemaphoreType.DMA((2,)),
        ],
        limit=60,
        ins="hhhhh",
        outs="h",
    )
    got = lax.all_to_all(sent, "expert", split_axis=0, concat_axis=0, tiled=True)
    piece = shape(z_chips, chunk, cols)
    back, own, *pieces = call(
        expert_kernel,
        [shape(block, PACK * width + LANES)] + [piece] * len(FIRST),
        (got, w_gate[0], w_up[0], w_down[0]),
        flops=16 * rows * width * hidden_units,
        scratch=[
            pltpu.VMEM((rows, width), BF16),
            pltpu.VMEM((rows, width), BF16),
            pltpu.VMEM((rows, cols), BF16),
            pltpu.VMEM((width // chunk, chunk, cols), BF16),
        ],
    )

    returned = lax.all_to_all(back, "expert", split_axis=0, concat_axis=0, tiled=True)
    arrived = [
        lax.ppermute(values, "x", [(i, (i + dx) % X_CHIPS) for i in range(X_CHIPS)])
        for values, dx in zip(pieces, FIRST[1:], strict=True)
    ]
    (summed,) = call(partial_kernel, [piece], (own, *arrived), limit=16)
    summed, returned = lax.optimization_barrier((summed, returned))
    parts = lax.all_to_all(summed, "z", split_axis=0, concat_axis=0, tiled=True)
    grad_tokens, grad_combine = call(
        functools.partial(combine_kernel, experts, per),
        [shape(tok_rows, width), shape(*ids_t.shape)],
        (returned, ids_t, slots_t),
        flops=2 * tok_rows * rows * width,
    )
    grads = call(total_kernel, [shape(chunk, hidden_units, dtype=F32)] * 3, (parts,))
    return grad_tokens, grad_combine.T, grads[0][None], grads[1][None], grads[2].T[None]


def solution(mesh):
    groups, experts = mesh.devices.shape
    split = Mesh(mesh.devices.reshape(groups // X_CHIPS, X_CHIPS, experts), ("z", "x", "expert"))
    dp = ("z", "x")
    rows = P((*dp, "expert"), None)
    weight = P("expert", None, None)
    return jax.shard_map(
        shards,
        mesh=split,
        in_specs=(rows,) * 5 + (weight,) * 3,
        out_specs=(rows, rows, P("expert", dp, None), P("expert", dp, None), P("expert", None, dp)),
        check_vma=False,
    )
```

```python
import functools

import jax
import jax.numpy as jnp
from jax import lax
from jax.experimental import pallas as pl
from jax.experimental.pallas import tpu as pltpu
from jax.sharding import Mesh, PartitionSpec as P

X_CHIPS = 4
LANES = 128
PACK = 4
CODE = LANES // PACK
LOW = 2
FIRST = ((0, 0), (2, 1), (2, 0), (0, 1), (1, 0), (3, 0), (1, 1), (3, 1))
F32 = jnp.float32
BF16 = jnp.bfloat16
NN = (((1,), (0,)), ((), ()))
TN = (((0,), (0,)), ((), ()))
NT = (((1,), (1,)), ((), ()))


def dot(a, b, dims=NN):
    return lax.dot_general(a, b, dims, preferred_element_type=F32)


def positions(ids, slots, experts, per):
    group = slots // per
    row = group * (experts * per) + ids * per + (slots - group * per)
    return jnp.where(slots >= 0, row, -1)


def dispatch_kernel(experts, per, x_hbm, g_hbm, c_hbm, id_hbm, slot_hbm, out_hbm,
                    x_ref, g_ref, c_ref, id_ref, slot_ref, out_ref, sems, out_sems):
    tokens, width = x_ref.shape
    block = experts * per
    rows = PACK * block
    fetches = [
        pltpu.make_async_copy(source, ref, sems.at[i])
        for i, (source, ref) in enumerate(
            ((id_hbm, id_ref), (slot_hbm, slot_ref), (c_hbm, c_ref), (x_hbm, x_ref), (g_hbm, g_ref))
        )
    ]
    for fetch in fetches:
        fetch.start()
    fetch_x, fetch_g = fetches[3:]
    for fetch in fetches[:3]:
        fetch.wait()
    pos = positions(id_ref[...], slot_ref[...], experts, per)
    weights = c_ref[...].astype(F32)
    index = lax.broadcasted_iota(jnp.int32, (rows, tokens), 0)
    routed = jnp.zeros((rows, tokens), F32)
    scaled = jnp.zeros((rows, tokens), F32)
    for k in range(pos.shape[0]):
        match = index == pos[k : k + 1, :]
        routed = jnp.where(match, 1.0, routed)
        scaled = jnp.where(match, weights[k : k + 1, :], scaled)
    routed = routed.astype(BF16)
    code = jnp.sum(scaled, axis=1, keepdims=True)
    lane = lax.broadcasted_iota(jnp.int32, (block, LANES), 1)
    coded = jnp.zeros((block, LANES), F32)
    for q in range(PACK):
        coded = jnp.where(lane // CODE == q, code[q * block : (q + 1) * block], coded)
    out_ref[:, 2 * PACK * width :] = coded.astype(BF16)
    fetch_x.wait()
    sends = []
    for i, (fetch, ref) in enumerate(((None, x_ref), (fetch_g, g_ref))):
        if fetch is not None:
            fetch.wait()
        for q in range(PACK):
            lo = (i * PACK + q) * width
            hi = lo + width if (i, q) != (1, PACK - 1) else out_ref.shape[1]
            out_ref[:, lo : lo + width] = dot(routed[q * block : (q + 1) * block], ref[...]).astype(BF16)
            sends.append(pltpu.make_async_copy(out_ref.at[:, lo:hi], out_hbm.at[:, lo:hi], out_sems.at[len(sends)]))
            sends[-1].start()
    for send in sends:
        send.wait()


def expert_kernel(rows_ref, wg_ref, wu_ref, wd_ref, back_hbm, *rest):
    pieces, (x_all, g_all, act_all, part, back_ref, sem) = rest[:-6], rest[-6:]
    block = back_ref.shape[0]
    hidden_units, width = wd_ref.shape
    rows = PACK * block
    for q in range(PACK):
        x_all[q * block : (q + 1) * block, :] = rows_ref[:, q * width : (q + 1) * width]
        g_all[q * block : (q + 1) * block, :] = rows_ref[:, (PACK + q) * width : (PACK + q + 1) * width]
    lane = lax.broadcasted_iota(jnp.int32, (block, LANES), 1)
    sums = jnp.zeros((block, LANES), F32)
    step = rows // 2
    for lo in range(0, rows, step):
        hi = lo + step
        g = g_all[lo:hi, :]
        c = jnp.concatenate(
            [
                rows_ref[:, 2 * PACK * width + q * CODE : 2 * PACK * width + q * CODE + 1].astype(F32)
                for q in range(lo // block, hi // block)
            ],
            axis=0,
        )
        gate = dot(x_all[lo:hi, :], wg_ref[...])
        up = dot(x_all[lo:hi, :], wu_ref[...])
        sig = 1.0 / (1.0 + jnp.exp(-gate))
        act = gate * sig
        hidden = (act * up).astype(BF16)
        g_hidden = dot(g, wd_ref[...], NT)
        row_combine = jnp.sum(hidden.astype(F32) * g_hidden, axis=1, keepdims=True)
        for q in range(lo // block, hi // block):
            sums = jnp.where(lane // CODE == q, row_combine[q * block - lo : (q + 1) * block - lo], sums)
        grad_hidden = c * g_hidden
        g_all[lo:hi, :] = (c * g.astype(F32)).astype(BF16)
        act_all[lo:hi, :hidden_units] = (grad_hidden * up * (sig * (1.0 + gate * (1.0 - sig)))).astype(BF16)
        act_all[lo:hi, hidden_units : 2 * hidden_units] = (grad_hidden * act).astype(BF16)
        act_all[lo:hi, 2 * hidden_units :] = hidden
    back_ref[:, PACK * width :] = sums.astype(BF16)
    grad = dot(act_all[:, :hidden_units], wg_ref[...], NT)
    grad = (grad + dot(act_all[:, hidden_units : 2 * hidden_units], wu_ref[...], NT)).astype(BF16)
    for q in range(PACK):
        back_ref[:, q * width : (q + 1) * width] = grad[q * block : (q + 1) * block]
    store = pltpu.make_async_copy(back_ref, back_hbm, sem)
    store.start()
    x_here, low_here = lax.axis_index("x"), lax.axis_index("zl")
    places = [lax.rem(low_here + dz, LOW) * X_CHIPS + lax.rem(x_here + dx, X_CHIPS) for dx, dz in FIRST]
    chunk = part.shape[2]
    step = chunk * len(FIRST)
    for z in range(width // step):
        lo, hi = z * step, (z + 1) * step
        upper = dot(x_all[:, lo:hi], act_all[:, : 2 * hidden_units], TN).astype(BF16)
        lower = dot(g_all[:, lo:hi], act_all[:, 2 * hidden_units :], TN).astype(BF16)
        for j in range(len(FIRST)):
            part[z, j, :, : 2 * hidden_units] = upper[j * chunk : (j + 1) * chunk]
            part[z, j, :, 2 * hidden_units :] = lower[j * chunk : (j + 1) * chunk]
        for place, ref in zip(places, pieces, strict=True):
            ref[z] = part[z, place]
    store.wait()


def partial_kernel(*refs):
    total = refs[0][...].astype(F32)
    for ref in refs[1:-1]:
        total = total + ref[...].astype(F32)
    refs[-1][...] = total.astype(BF16)


def combine_kernel(experts, per, back_ref, id_ref, slot_ref, grad_ref, comb_ref):
    tokens, width = grad_ref.shape
    block = experts * per
    rows = PACK * block
    pos = positions(id_ref[...], slot_ref[...], experts, per)
    index = lax.broadcasted_iota(jnp.int32, (rows, tokens), 0)
    code = jnp.concatenate(
        [
            back_ref[:, PACK * width + q * CODE : PACK * width + q * CODE + 1].astype(F32)
            for q in range(PACK)
        ],
        axis=0,
    )
    routed = jnp.zeros((rows, tokens), F32)
    choice = lax.broadcasted_iota(jnp.int32, pos.shape, 0)
    comb = jnp.zeros(pos.shape, F32)
    for k in range(pos.shape[0]):
        match = index == pos[k : k + 1, :]
        routed = jnp.where(match, 1.0, routed)
        value = jnp.sum(jnp.where(match, code, 0.0), axis=0, keepdims=True)
        comb = jnp.where(choice == k, value, comb)
    comb_ref[...] = comb.astype(BF16)
    routed = routed.astype(BF16)
    grad = jnp.zeros((tokens, width), F32)
    for q in range(PACK):
        grad = grad + dot(routed[q * block : (q + 1) * block], back_ref[:, q * width : (q + 1) * width], TN)
    grad_ref[...] = grad.astype(BF16)


def total_kernel(parts_ref, gate_ref, up_ref, down_ref):
    hidden_units = gate_ref.shape[1]
    total = jnp.sum(parts_ref[...].astype(F32), axis=0)
    gate_ref[...] = total[:, :hidden_units]
    up_ref[...] = total[:, hidden_units : 2 * hidden_units]
    down_ref[...] = total[:, 2 * hidden_units :]


def call(kernel, out_shape, args, flops=0, scratch=(), limit=24, ins="", outs=""):
    moved = sum(a.size * a.dtype.itemsize for a in (*args, *out_shape))

    def specs(letters, count):
        letters = letters.ljust(count, "v")
        return [pl.BlockSpec(memory_space=pltpu.HBM if c == "h" else pltpu.VMEM) for c in letters]

    return pl.pallas_call(
        kernel,
        out_shape=out_shape,
        in_specs=specs(ins, len(args)),
        out_specs=specs(outs, len(out_shape)),
        scratch_shapes=scratch,
        compiler_params=pltpu.CompilerParams(vmem_limit_bytes=limit << 20),
        cost_estimate=pl.CostEstimate(flops=flops, bytes_accessed=moved, transcendentals=0),
    )(*args)


def shape(*dims, dtype=BF16):
    return jax.ShapeDtypeStruct(dims, dtype)


def shards(tokens, grad_out, combine, expert_ids, slots, w_gate, w_up, w_down):
    tok_rows, width = tokens.shape
    hidden_units = w_gate.shape[2]
    experts = lax.axis_size("expert")
    high = lax.axis_size("zh")
    per = tok_rows // 8 // PACK
    block = experts * per
    rows = PACK * block
    chunk = width // (high * LOW * X_CHIPS)
    cols = 3 * hidden_units
    ids_t, slots_t, combine_t = expert_ids.T, slots.T, combine.T

    (sent,) = call(
        functools.partial(dispatch_kernel, experts, per),
        [shape(block, 2 * PACK * width + LANES)],
        (tokens, grad_out, combine_t, ids_t, slots_t),
        flops=4 * tok_rows * rows * width,
        scratch=[
            pltpu.VMEM((tok_rows, width), BF16),
            pltpu.VMEM((tok_rows, width), BF16),
            pltpu.VMEM(combine_t.shape, BF16),
            pltpu.VMEM(ids_t.shape, jnp.int32),
            pltpu.VMEM(slots_t.shape, jnp.int32),
            pltpu.VMEM((block, 2 * PACK * width + LANES), BF16),
            pltpu.SemaphoreType.DMA((5,)),
            pltpu.SemaphoreType.DMA((2 * PACK,)),
        ],
        limit=60,
        ins="hhhhh",
        outs="h",
    )
    got = lax.all_to_all(sent, "expert", split_axis=0, concat_axis=0, tiled=True)
    piece = shape(high, chunk, cols)
    back, own, *pieces = call(
        expert_kernel,
        [shape(block, PACK * width + LANES)] + [piece] * len(FIRST),
        (got, w_gate[0], w_up[0], w_down[0]),
        flops=16 * rows * width * hidden_units,
        scratch=[
            pltpu.VMEM((rows, width), BF16),
            pltpu.VMEM((rows, width), BF16),
            pltpu.VMEM((rows, cols), BF16),
            pltpu.VMEM((high, len(FIRST), chunk, cols), BF16),
            pltpu.VMEM((block, PACK * width + LANES), BF16),
            pltpu.SemaphoreType.DMA,
        ],
        outs="h",
    )

    def shift(values, dx, dz):
        pairs = [
            (z * X_CHIPS + x, (z + dz) % LOW * X_CHIPS + (x + dx) % X_CHIPS)
            for z in range(LOW)
            for x in range(X_CHIPS)
        ]
        return lax.ppermute(values, ("zl", "x"), pairs)

    returned = lax.all_to_all(back, "expert", split_axis=0, concat_axis=0, tiled=True)
    arrived = [shift(values, dx, dz) for values, (dx, dz) in zip(pieces, FIRST[1:], strict=True)]
    (summed,) = call(partial_kernel, [piece], (own, *arrived), limit=16)
    summed, returned = lax.optimization_barrier((summed, returned))
    parts = lax.all_to_all(summed, "zh", split_axis=0, concat_axis=0, tiled=True)
    grad_tokens, grad_combine = call(
        functools.partial(combine_kernel, experts, per),
        [shape(tok_rows, width), shape(*ids_t.shape)],
        (returned, ids_t, slots_t),
        flops=2 * tok_rows * rows * width,
    )
    grads = call(total_kernel, [shape(chunk, hidden_units, dtype=F32)] * 3, (parts,))
    return grad_tokens, grad_combine.T, grads[0][None], grads[1][None], grads[2].T[None]


def solution(mesh):
    groups, experts = mesh.devices.shape
    split = Mesh(
        mesh.devices.reshape(groups // X_CHIPS // LOW, LOW, X_CHIPS, experts), ("zh", "zl", "x", "expert")
    )
    dp = ("zh", "zl", "x")
    rows = P((*dp, "expert"), None)
    weight = P("expert", None, None)
    return jax.shard_map(
        shards,
        mesh=split,
        in_specs=(rows,) * 5 + (weight,) * 3,
        out_specs=(rows, rows, P("expert", dp, None), P("expert", dp, None), P("expert", None, dp)),
        check_vma=False,
    )
```

```python
import functools

import jax
import jax.numpy as jnp
from jax import lax
from jax.experimental import pallas as pl
from jax.experimental.pallas import tpu as pltpu
from jax.sharding import Mesh, PartitionSpec as P

X_CHIPS = 4
LANES = 128
PACK = 4
CODE = LANES // PACK
LOW = 2
FIRST = ((0, 0), (2, 1), (2, 0), (0, 1), (1, 0), (3, 0), (1, 1), (3, 1))
F32 = jnp.float32
BF16 = jnp.bfloat16
NN = (((1,), (0,)), ((), ()))
TN = (((0,), (0,)), ((), ()))
NT = (((1,), (1,)), ((), ()))


def dot(a, b, dims=NN):
    return lax.dot_general(a, b, dims, preferred_element_type=F32)


def positions(ids, slots, experts, per):
    group = slots // per
    row = group * (experts * per) + ids * per + (slots - group * per)
    return jnp.where(slots >= 0, row, -1)


def dispatch_kernel(experts, per, x_hbm, g_hbm, c_hbm, id_hbm, slot_hbm, out_hbm,
                    x_ref, g_ref, c_ref, id_ref, slot_ref, out_ref, sems, out_sems):
    tokens, width = x_ref.shape
    block = experts * per
    rows = PACK * block
    fetches = [
        pltpu.make_async_copy(source, ref, sems.at[i])
        for i, (source, ref) in enumerate(
            ((id_hbm, id_ref), (slot_hbm, slot_ref), (c_hbm, c_ref), (x_hbm, x_ref), (g_hbm, g_ref))
        )
    ]
    for fetch in fetches:
        fetch.start()
    fetch_x, fetch_g = fetches[3:]
    for fetch in fetches[:3]:
        fetch.wait()
    pos = positions(id_ref[...], slot_ref[...], experts, per)
    weights = c_ref[...].astype(F32)
    index = lax.broadcasted_iota(jnp.int32, (block, tokens), 0)
    lane = lax.broadcasted_iota(jnp.int32, (block, LANES), 1)
    coded = jnp.zeros((block, LANES), F32)
    picks, sends = [], []

    def send(lo, hi):
        copy = pltpu.make_async_copy(out_ref.at[:, lo:hi], out_hbm.at[:, lo:hi], out_sems.at[len(sends)])
        copy.start()
        sends.append(copy)

    for q in range(PACK):
        routed = jnp.zeros((block, tokens), F32)
        scaled = jnp.zeros((block, tokens), F32)
        for k in range(pos.shape[0]):
            match = index + q * block == pos[k : k + 1, :]
            routed = jnp.where(match, 1.0, routed)
            scaled = jnp.where(match, weights[k : k + 1, :], scaled)
        picks.append(routed.astype(BF16))
        coded = jnp.where(lane // CODE == q, jnp.sum(scaled, axis=1, keepdims=True), coded)
        if q == 0:
            fetch_x.wait()
        out_ref[:, q * width : (q + 1) * width] = dot(picks[q], x_ref[...]).astype(BF16)
        send(q * width, (q + 1) * width)
    out_ref[:, 2 * PACK * width :] = coded.astype(BF16)
    fetch_g.wait()
    for q in range(PACK):
        lo = (PACK + q) * width
        out_ref[:, lo : lo + width] = dot(picks[q], g_ref[...]).astype(BF16)
        send(lo, lo + width if q < PACK - 1 else out_ref.shape[1])
    for copy in sends:
        copy.wait()


def expert_kernel(rows_ref, wg_ref, wu_ref, wd_ref, back_hbm, *rest):
    pieces, (wgu_ref, x_all, g_all, act_all, part, back_ref, sem) = rest[:-7], rest[-7:]
    block = back_ref.shape[0]
    hidden_units, width = wd_ref.shape
    rows = PACK * block
    wgu_ref[:, :hidden_units] = wg_ref[...]
    wgu_ref[:, hidden_units:] = wu_ref[...]
    for q in range(PACK):
        x_all[q * block : (q + 1) * block, :] = rows_ref[:, q * width : (q + 1) * width]
        g_all[q * block : (q + 1) * block, :] = rows_ref[:, (PACK + q) * width : (PACK + q + 1) * width]
    lane = lax.broadcasted_iota(jnp.int32, (block, LANES), 1)
    sums = jnp.zeros((block, LANES), F32)
    step = rows // 2
    for lo in range(0, rows, step):
        hi = lo + step
        g = g_all[lo:hi, :]
        c = jnp.concatenate(
            [
                rows_ref[:, 2 * PACK * width + q * CODE : 2 * PACK * width + q * CODE + 1].astype(F32)
                for q in range(lo // block, hi // block)
            ],
            axis=0,
        )
        pre = dot(x_all[lo:hi, :], wgu_ref[...])
        gate, up = pre[:, :hidden_units], pre[:, hidden_units:]
        sig = 1.0 / (1.0 + jnp.exp(-gate))
        act = gate * sig
        hidden = (act * up).astype(BF16)
        g_hidden = dot(g, wd_ref[...], NT)
        row_combine = jnp.sum(hidden.astype(F32) * g_hidden, axis=1, keepdims=True)
        for q in range(lo // block, hi // block):
            sums = jnp.where(lane // CODE == q, row_combine[q * block - lo : (q + 1) * block - lo], sums)
        grad_hidden = c * g_hidden
        g_all[lo:hi, :] = (c * g.astype(F32)).astype(BF16)
        act_all[lo:hi, :hidden_units] = (grad_hidden * up * (sig * (1.0 + gate * (1.0 - sig)))).astype(BF16)
        act_all[lo:hi, hidden_units : 2 * hidden_units] = (grad_hidden * act).astype(BF16)
        act_all[lo:hi, 2 * hidden_units :] = hidden
    back_ref[:, PACK * width :] = sums.astype(BF16)
    grad = dot(act_all[:, : 2 * hidden_units], wgu_ref[...], NT).astype(BF16)
    for q in range(PACK):
        back_ref[:, q * width : (q + 1) * width] = grad[q * block : (q + 1) * block]
    store = pltpu.make_async_copy(back_ref, back_hbm, sem)
    store.start()
    x_here, low_here = lax.axis_index("x"), lax.axis_index("zl")
    flips = (x_here, x_here + 1 - 2 * lax.rem(x_here, 2), lax.rem(x_here + 2, X_CHIPS), X_CHIPS - 1 - x_here)
    places = [lax.rem(low_here + dz, LOW) * X_CHIPS + flips[dx] for dx, dz in FIRST]
    chunk = part.shape[2]
    step = chunk * len(FIRST)
    for z in range(width // step):
        lo, hi = z * step, (z + 1) * step
        upper = dot(x_all[:, lo:hi], act_all[:, : 2 * hidden_units], TN).astype(BF16)
        lower = dot(g_all[:, lo:hi], act_all[:, 2 * hidden_units :], TN).astype(BF16)
        for j in range(len(FIRST)):
            part[z, j, :, : 2 * hidden_units] = upper[j * chunk : (j + 1) * chunk]
            part[z, j, :, 2 * hidden_units :] = lower[j * chunk : (j + 1) * chunk]
        for place, ref in zip(places, pieces, strict=True):
            ref[z] = part[z, place]
    store.wait()


def partial_kernel(*refs):
    parts, (out_hbm, out_ref, sems) = refs[:-3], refs[-3:]
    stores = []
    for z in range(out_ref.shape[0]):
        total = parts[0][z].astype(F32)
        for ref in parts[1:]:
            total = total + ref[z].astype(F32)
        out_ref[z] = total.astype(BF16)
        stores.append(pltpu.make_async_copy(out_ref.at[z], out_hbm.at[z], sems.at[z]))
        stores[-1].start()
    for store in stores:
        store.wait()


def combine_kernel(experts, per, back_ref, id_ref, slot_ref, grad_ref, comb_ref):
    tokens, width = grad_ref.shape
    block = experts * per
    rows = PACK * block
    pos = positions(id_ref[...], slot_ref[...], experts, per)
    index = lax.broadcasted_iota(jnp.int32, (rows, tokens), 0)
    code = jnp.concatenate(
        [
            back_ref[:, PACK * width + q * CODE : PACK * width + q * CODE + 1].astype(F32)
            for q in range(PACK)
        ],
        axis=0,
    )
    routed = jnp.zeros((rows, tokens), F32)
    choice = lax.broadcasted_iota(jnp.int32, pos.shape, 0)
    comb = jnp.zeros(pos.shape, F32)
    for k in range(pos.shape[0]):
        match = index == pos[k : k + 1, :]
        routed = jnp.where(match, 1.0, routed)
        value = jnp.sum(jnp.where(match, code, 0.0), axis=0, keepdims=True)
        comb = jnp.where(choice == k, value, comb)
    comb_ref[...] = comb.astype(BF16)
    routed = routed.astype(BF16)
    grad = jnp.zeros((tokens, width), F32)
    for q in range(PACK):
        grad = grad + dot(routed[q * block : (q + 1) * block], back_ref[:, q * width : (q + 1) * width], TN)
    grad_ref[...] = grad.astype(BF16)


def total_kernel(parts_ref, gate_ref, up_ref, down_ref):
    hidden_units = gate_ref.shape[1]
    total = jnp.sum(parts_ref[...].astype(F32), axis=0)
    gate_ref[...] = total[:, :hidden_units]
    up_ref[...] = total[:, hidden_units : 2 * hidden_units]
    down_ref[...] = total[:, 2 * hidden_units :]


def call(kernel, out_shape, args, flops=0, scratch=(), limit=24, ins="", outs=""):
    moved = sum(a.size * a.dtype.itemsize for a in (*args, *out_shape))

    def specs(letters, count):
        letters = letters.ljust(count, "v")
        return [pl.BlockSpec(memory_space=pltpu.HBM if c == "h" else pltpu.VMEM) for c in letters]

    return pl.pallas_call(
        kernel,
        out_shape=out_shape,
        in_specs=specs(ins, len(args)),
        out_specs=specs(outs, len(out_shape)),
        scratch_shapes=scratch,
        compiler_params=pltpu.CompilerParams(vmem_limit_bytes=limit << 20),
        cost_estimate=pl.CostEstimate(flops=flops, bytes_accessed=moved, transcendentals=0),
    )(*args)


def shape(*dims, dtype=BF16):
    return jax.ShapeDtypeStruct(dims, dtype)


def shards(tokens, grad_out, combine, expert_ids, slots, w_gate, w_up, w_down):
    tok_rows, width = tokens.shape
    hidden_units = w_gate.shape[2]
    experts = lax.axis_size("expert")
    high = lax.axis_size("zh")
    per = tok_rows // 8 // PACK
    block = experts * per
    rows = PACK * block
    chunk = width // (high * LOW * X_CHIPS)
    cols = 3 * hidden_units
    ids_t, slots_t, combine_t = expert_ids.T, slots.T, combine.T

    (sent,) = call(
        functools.partial(dispatch_kernel, experts, per),
        [shape(block, 2 * PACK * width + LANES)],
        (tokens, grad_out, combine_t, ids_t, slots_t),
        flops=4 * tok_rows * rows * width,
        scratch=[
            pltpu.VMEM((tok_rows, width), BF16),
            pltpu.VMEM((tok_rows, width), BF16),
            pltpu.VMEM(combine_t.shape, BF16),
            pltpu.VMEM(ids_t.shape, jnp.int32),
            pltpu.VMEM(slots_t.shape, jnp.int32),
            pltpu.VMEM((block, 2 * PACK * width + LANES), BF16),
            pltpu.SemaphoreType.DMA((5,)),
            pltpu.SemaphoreType.DMA((2 * PACK,)),
        ],
        limit=60,
        ins="hhhhh",
        outs="h",
    )
    got = lax.all_to_all(sent, "expert", split_axis=0, concat_axis=0, tiled=True)
    piece = shape(high, chunk, cols)
    back, own, *pieces = call(
        expert_kernel,
        [shape(block, PACK * width + LANES)] + [piece] * len(FIRST),
        (got, w_gate[0], w_up[0], w_down[0]),
        flops=16 * rows * width * hidden_units,
        scratch=[
            pltpu.VMEM((width, 2 * hidden_units), BF16),
            pltpu.VMEM((rows, width), BF16),
            pltpu.VMEM((rows, width), BF16),
            pltpu.VMEM((rows, cols), BF16),
            pltpu.VMEM((high, len(FIRST), chunk, cols), BF16),
            pltpu.VMEM((block, PACK * width + LANES), BF16),
            pltpu.SemaphoreType.DMA,
        ],
        outs="h",
    )

    def shift(values, dx, dz):
        pairs = [
            (z * X_CHIPS + x, (z ^ dz) * X_CHIPS + (x ^ dx))
            for z in range(LOW)
            for x in range(X_CHIPS)
        ]
        return lax.ppermute(values, ("zl", "x"), pairs)

    returned = lax.all_to_all(back, "expert", split_axis=0, concat_axis=0, tiled=True)
    arrived = [shift(values, dx, dz) for values, (dx, dz) in zip(pieces, FIRST[1:], strict=True)]
    (summed,) = call(
        partial_kernel,
        [piece],
        (own, *arrived),
        scratch=[pltpu.VMEM(piece.shape, BF16), pltpu.SemaphoreType.DMA((high,))],
        limit=16,
        outs="h",
    )
    summed, returned = lax.optimization_barrier((summed, returned))
    parts = lax.all_to_all(summed, "zh", split_axis=0, concat_axis=0, tiled=True)
    grad_tokens, grad_combine = call(
        functools.partial(combine_kernel, experts, per),
        [shape(tok_rows, width), shape(*ids_t.shape)],
        (returned, ids_t, slots_t),
        flops=2 * tok_rows * rows * width,
    )
    grads = call(total_kernel, [shape(chunk, hidden_units, dtype=F32)] * 3, (parts,))
    return grad_tokens, grad_combine.T, grads[0][None], grads[1][None], grads[2].T[None]


def solution(mesh):
    groups, experts = mesh.devices.shape
    split = Mesh(
        mesh.devices.reshape(groups // X_CHIPS // LOW, LOW, X_CHIPS, experts), ("zh", "zl", "x", "expert")
    )
    dp = ("zh", "zl", "x")
    rows = P((*dp, "expert"), None)
    weight = P("expert", None, None)
    return jax.shard_map(
        shards,
        mesh=split,
        in_specs=(rows,) * 5 + (weight,) * 3,
        out_specs=(rows, rows, P("expert", dp, None), P("expert", dp, None), P("expert", None, dp)),
        check_vma=False,
    )
```

```python
import functools

import jax
import jax.numpy as jnp
from jax import lax
from jax.experimental import pallas as pl
from jax.experimental.pallas import tpu as pltpu
from jax.sharding import Mesh, PartitionSpec as P

X_CHIPS = 4
LANES = 128
PACK = 4
CODE = LANES // PACK
LOW = 2
FIRST = ((0, 0), (2, 1), (2, 0), (0, 1), (3, 0), (1, 1), (1, 0), (3, 1))
F32 = jnp.float32
BF16 = jnp.bfloat16
NN = (((1,), (0,)), ((), ()))
TN = (((0,), (0,)), ((), ()))
NT = (((1,), (1,)), ((), ()))


def dot(a, b, dims=NN):
    return lax.dot_general(a, b, dims, preferred_element_type=F32)


def positions(ids, slots, experts, per):
    group = slots // per
    row = group * (experts * per) + ids * per + (slots - group * per)
    return jnp.where(slots >= 0, row, -1)


def dispatch_kernel(experts, per, x_hbm, g_hbm, c_hbm, id_hbm, slot_hbm, out_hbm,
                    x_ref, g_ref, c_ref, id_ref, slot_ref, out_ref, sems, out_sems):
    tokens, width = x_ref.shape
    block = experts * per
    rows = PACK * block
    fetches = [
        pltpu.make_async_copy(source, ref, sems.at[i])
        for i, (source, ref) in enumerate(
            ((id_hbm, id_ref), (slot_hbm, slot_ref), (c_hbm, c_ref), (x_hbm, x_ref), (g_hbm, g_ref))
        )
    ]
    for fetch in fetches:
        fetch.start()
    fetch_x, fetch_g = fetches[3:]
    for fetch in fetches[:3]:
        fetch.wait()
    pos = positions(id_ref[...], slot_ref[...], experts, per)
    weights = c_ref[...].astype(F32)
    index = lax.broadcasted_iota(jnp.int32, (block, tokens), 0)
    lane = lax.broadcasted_iota(jnp.int32, (block, LANES), 1)
    coded = jnp.zeros((block, LANES), F32)
    picks, sends = [], []

    def send(lo, hi):
        copy = pltpu.make_async_copy(out_ref.at[:, lo:hi], out_hbm.at[:, lo:hi], out_sems.at[len(sends)])
        copy.start()
        sends.append(copy)

    for q in range(PACK):
        routed = jnp.zeros((block, tokens), F32)
        scaled = jnp.zeros((block, tokens), F32)
        for k in range(pos.shape[0]):
            match = index + q * block == pos[k : k + 1, :]
            routed = jnp.where(match, 1.0, routed)
            scaled = jnp.where(match, weights[k : k + 1, :], scaled)
        picks.append(routed.astype(BF16))
        coded = jnp.where(lane // CODE == q, jnp.sum(scaled, axis=1, keepdims=True), coded)
        if q == 0:
            fetch_x.wait()
        out_ref[:, q * width : (q + 1) * width] = dot(picks[q], x_ref[...]).astype(BF16)
        send(q * width, (q + 1) * width)
    out_ref[:, 2 * PACK * width :] = coded.astype(BF16)
    fetch_g.wait()
    for q in range(PACK):
        lo = (PACK + q) * width
        out_ref[:, lo : lo + width] = dot(picks[q], g_ref[...]).astype(BF16)
        send(lo, lo + width if q < PACK - 1 else out_ref.shape[1])
    for copy in sends:
        copy.wait()


def expert_kernel(rows_ref, wg_ref, wu_ref, wd_ref, back_hbm, *rest):
    pieces, (wgu_ref, x_all, g_all, act_all, part, back_ref, sem) = rest[:-7], rest[-7:]
    block = back_ref.shape[0]
    hidden_units, width = wd_ref.shape
    rows = PACK * block
    wgu_ref[:, :hidden_units] = wg_ref[...]
    wgu_ref[:, hidden_units:] = wu_ref[...]
    for q in range(PACK):
        x_all[q * block : (q + 1) * block, :] = rows_ref[:, q * width : (q + 1) * width]
        g_all[q * block : (q + 1) * block, :] = rows_ref[:, (PACK + q) * width : (PACK + q + 1) * width]
    lane = lax.broadcasted_iota(jnp.int32, (block, LANES), 1)
    sums = jnp.zeros((block, LANES), F32)
    step = rows // 2
    for lo in range(0, rows, step):
        hi = lo + step
        g = g_all[lo:hi, :]
        c = jnp.concatenate(
            [
                rows_ref[:, 2 * PACK * width + q * CODE : 2 * PACK * width + q * CODE + 1].astype(F32)
                for q in range(lo // block, hi // block)
            ],
            axis=0,
        )
        pre = dot(x_all[lo:hi, :], wgu_ref[...])
        gate, up = pre[:, :hidden_units], pre[:, hidden_units:]
        sig = 1.0 / (1.0 + jnp.exp(-gate))
        act = gate * sig
        hidden = (act * up).astype(BF16)
        g_hidden = dot(g, wd_ref[...], NT)
        row_combine = jnp.sum(hidden.astype(F32) * g_hidden, axis=1, keepdims=True)
        for q in range(lo // block, hi // block):
            sums = jnp.where(lane // CODE == q, row_combine[q * block - lo : (q + 1) * block - lo], sums)
        grad_hidden = c * g_hidden
        g_all[lo:hi, :] = (c * g.astype(F32)).astype(BF16)
        act_all[lo:hi, :hidden_units] = (grad_hidden * up * (sig * (1.0 + gate * (1.0 - sig)))).astype(BF16)
        act_all[lo:hi, hidden_units : 2 * hidden_units] = (grad_hidden * act).astype(BF16)
        act_all[lo:hi, 2 * hidden_units :] = hidden
    back_ref[:, PACK * width :] = sums.astype(BF16)
    grad = dot(act_all[:, : 2 * hidden_units], wgu_ref[...], NT).astype(BF16)
    for q in range(PACK):
        back_ref[:, q * width : (q + 1) * width] = grad[q * block : (q + 1) * block]
    store = pltpu.make_async_copy(back_ref, back_hbm, sem)
    store.start()
    x_here, low_here = lax.axis_index("x"), lax.axis_index("zl")
    flips = (x_here, x_here + 1 - 2 * lax.rem(x_here, 2), lax.rem(x_here + 2, X_CHIPS), X_CHIPS - 1 - x_here)
    places = [lax.rem(low_here + dz, LOW) * X_CHIPS + flips[dx] for dx, dz in FIRST]
    chunk = part.shape[2]
    step = chunk * len(FIRST)
    for z in range(width // step):
        lo, hi = z * step, (z + 1) * step
        upper = dot(x_all[:, lo:hi], act_all[:, : 2 * hidden_units], TN).astype(BF16)
        lower = dot(g_all[:, lo:hi], act_all[:, 2 * hidden_units :], TN).astype(BF16)
        for j in range(len(FIRST)):
            part[z, j, :, : 2 * hidden_units] = upper[j * chunk : (j + 1) * chunk]
            part[z, j, :, 2 * hidden_units :] = lower[j * chunk : (j + 1) * chunk]
        for place, ref in zip(places, pieces, strict=True):
            ref[z] = part[z, place]
    store.wait()


def partial_kernel(*refs):
    parts, (out_hbm, out_ref, sems) = refs[:-3], refs[-3:]
    stores = []
    for z in range(out_ref.shape[0]):
        total = parts[0][z].astype(F32)
        for ref in parts[1:]:
            total = total + ref[z].astype(F32)
        out_ref[z] = total.astype(BF16)
        stores.append(pltpu.make_async_copy(out_ref.at[z], out_hbm.at[z], sems.at[z]))
        stores[-1].start()
    for store in stores:
        store.wait()


def combine_kernel(experts, per, back_ref, id_ref, slot_ref, grad_ref, comb_ref):
    tokens, width = grad_ref.shape
    block = experts * per
    rows = PACK * block
    pos = positions(id_ref[...], slot_ref[...], experts, per)
    index = lax.broadcasted_iota(jnp.int32, (rows, tokens), 0)
    code = jnp.concatenate(
        [
            back_ref[:, PACK * width + q * CODE : PACK * width + q * CODE + 1].astype(F32)
            for q in range(PACK)
        ],
        axis=0,
    )
    routed = jnp.zeros((rows, tokens), F32)
    choice = lax.broadcasted_iota(jnp.int32, pos.shape, 0)
    comb = jnp.zeros(pos.shape, F32)
    for k in range(pos.shape[0]):
        match = index == pos[k : k + 1, :]
        routed = jnp.where(match, 1.0, routed)
        value = jnp.sum(jnp.where(match, code, 0.0), axis=0, keepdims=True)
        comb = jnp.where(choice == k, value, comb)
    comb_ref[...] = comb.astype(BF16)
    routed = routed.astype(BF16)
    grad = jnp.zeros((tokens, width), F32)
    for q in range(PACK):
        grad = grad + dot(routed[q * block : (q + 1) * block], back_ref[:, q * width : (q + 1) * width], TN)
    grad_ref[...] = grad.astype(BF16)


def total_kernel(parts_ref, gate_ref, up_ref, down_ref):
    hidden_units = gate_ref.shape[1]
    total = jnp.sum(parts_ref[...].astype(F32), axis=0)
    gate_ref[...] = total[:, :hidden_units]
    up_ref[...] = total[:, hidden_units : 2 * hidden_units]
    down_ref[...] = total[:, 2 * hidden_units :]


def call(kernel, out_shape, args, flops=0, scratch=(), limit=24, ins="", outs=""):
    moved = sum(a.size * a.dtype.itemsize for a in (*args, *out_shape))

    def specs(letters, count):
        letters = letters.ljust(count, "v")
        return [pl.BlockSpec(memory_space=pltpu.HBM if c == "h" else pltpu.VMEM) for c in letters]

    return pl.pallas_call(
        kernel,
        out_shape=out_shape,
        in_specs=specs(ins, len(args)),
        out_specs=specs(outs, len(out_shape)),
        scratch_shapes=scratch,
        compiler_params=pltpu.CompilerParams(vmem_limit_bytes=limit << 20),
        cost_estimate=pl.CostEstimate(flops=flops, bytes_accessed=moved, transcendentals=0),
    )(*args)


def shape(*dims, dtype=BF16):
    return jax.ShapeDtypeStruct(dims, dtype)


def shards(tokens, grad_out, combine, expert_ids, slots, w_gate, w_up, w_down):
    tok_rows, width = tokens.shape
    hidden_units = w_gate.shape[2]
    experts = lax.axis_size("expert")
    high = lax.axis_size("zh")
    per = tok_rows // 8 // PACK
    block = experts * per
    rows = PACK * block
    chunk = width // (high * LOW * X_CHIPS)
    cols = 3 * hidden_units
    ids_t, slots_t, combine_t = expert_ids.T, slots.T, combine.T

    (sent,) = call(
        functools.partial(dispatch_kernel, experts, per),
        [shape(block, 2 * PACK * width + LANES)],
        (tokens, grad_out, combine_t, ids_t, slots_t),
        flops=4 * tok_rows * rows * width,
        scratch=[
            pltpu.VMEM((tok_rows, width), BF16),
            pltpu.VMEM((tok_rows, width), BF16),
            pltpu.VMEM(combine_t.shape, BF16),
            pltpu.VMEM(ids_t.shape, jnp.int32),
            pltpu.VMEM(slots_t.shape, jnp.int32),
            pltpu.VMEM((block, 2 * PACK * width + LANES), BF16),
            pltpu.SemaphoreType.DMA((5,)),
            pltpu.SemaphoreType.DMA((2 * PACK,)),
        ],
        limit=60,
        ins="hhhhh",
        outs="h",
    )
    got = lax.all_to_all(sent, "expert", split_axis=0, concat_axis=0, tiled=True)
    piece = shape(high, chunk, cols)
    back, own, *pieces = call(
        expert_kernel,
        [shape(block, PACK * width + LANES)] + [piece] * len(FIRST),
        (got, w_gate[0], w_up[0], w_down[0]),
        flops=16 * rows * width * hidden_units,
        scratch=[
            pltpu.VMEM((width, 2 * hidden_units), BF16),
            pltpu.VMEM((rows, width), BF16),
            pltpu.VMEM((rows, width), BF16),
            pltpu.VMEM((rows, cols), BF16),
            pltpu.VMEM((high, len(FIRST), chunk, cols), BF16),
            pltpu.VMEM((block, PACK * width + LANES), BF16),
            pltpu.SemaphoreType.DMA,
        ],
        outs="h",
    )

    def shift(values, dx, dz):
        pairs = [
            (z * X_CHIPS + x, (z ^ dz) * X_CHIPS + (x ^ dx))
            for z in range(LOW)
            for x in range(X_CHIPS)
        ]
        return lax.ppermute(values, ("zl", "x"), pairs)

    returned = lax.all_to_all(back, "expert", split_axis=0, concat_axis=0, tiled=True)
    arrived = [shift(values, dx, dz) for values, (dx, dz) in zip(pieces, FIRST[1:], strict=True)]
    (summed,) = call(
        partial_kernel,
        [piece],
        (own, *arrived),
        scratch=[pltpu.VMEM(piece.shape, BF16), pltpu.SemaphoreType.DMA((high,))],
        limit=16,
        outs="h",
    )
    summed, returned = lax.optimization_barrier((summed, returned))
    parts = lax.all_to_all(summed, "zh", split_axis=0, concat_axis=0, tiled=True)
    grad_tokens, grad_combine = call(
        functools.partial(combine_kernel, experts, per),
        [shape(tok_rows, width), shape(*ids_t.shape)],
        (returned, ids_t, slots_t),
        flops=2 * tok_rows * rows * width,
    )
    grads = call(total_kernel, [shape(chunk, hidden_units, dtype=F32)] * 3, (parts,))
    return grad_tokens, grad_combine.T, grads[0][None], grads[1][None], grads[2].T[None]


def solution(mesh):
    groups, experts = mesh.devices.shape
    split = Mesh(
        mesh.devices.reshape(groups // X_CHIPS // LOW, LOW, X_CHIPS, experts), ("zh", "zl", "x", "expert")
    )
    dp = ("zh", "zl", "x")
    rows = P((*dp, "expert"), None)
    weight = P("expert", None, None)
    return jax.shard_map(
        shards,
        mesh=split,
        in_specs=(rows,) * 5 + (weight,) * 3,
        out_specs=(rows, rows, P("expert", dp, None), P("expert", dp, None), P("expert", None, dp)),
        check_vma=False,
    )
```
